128 devices in a mesh: prompt: 4 (over z_hi, core), sample: 32 (over x, z_lo, y).
Axes of the slice: x: 4, y: 4, z: 4 (z_hi: 2, z_lo: 2; z = z_hi * 2 + z_lo), core: 2. Of those that a mesh axis runs over, the one named last changes fastest.
Arguments:
- answer_qkv: bfloat16 [4, 4096, 3, 4096], P('prompt', 'sample'), may hold values from -80 to 80
- prefix_kv: bfloat16 [4, 2048, 2, 4096], P(None, 'prompt', None, 'sample'), may hold values from -6 to 6
- reveal_qkv: bfloat16 [4, 512, 3, 4096], P('prompt', 'sample'), may hold values from -4 to 4
- reveal_places: int32 [4, 32, 16], P('prompt', 'sample'), may hold values from 0 to 127, as said below
Outputs:
- attended_one: bfloat16 [4, 4096, 4096], P('prompt', 'sample')
- attended_two: bfloat16 [4, 4096, 4096], P('prompt', 'sample')
The draws below stay inside these ranges and needn't reach their ends.
Inputs may be any that keep to these rules, and one draw needn't show every extreme that they name: `reveal_places`: within each prompt and segment the 16 entries are distinct positions of that segment.
All inputs are finite; a program needn't handle non-finite values.
Results may differ from the reference program's by a relative error of at most 0.0095.
Values may be sent and summed in bfloat16 or wider, within the bound.
No kernel may reach another device: no remote copies, remote signals or barrier semaphores. Data moves between devices by JAX's collectives and lax.ppermute only.
A program may use at most 128 MiB of HBM per device.

```python
import math
import jax
import jax.numpy as jnp
from jax import lax

HEADS = 32
HEAD_DIM = 128
PREFIX = 2048
ANS = 1024
SEG = 128
REV = 16
PROMPTS = 4
HD = 4096
TOK_P = 4096
SAMPLES = 4
SEGS_P = 32
REVROWS = 512


def draw_answer_qkv(key, part):
    key = jax.random.fold_in(key, 11)
    key_base, key_scale = jax.random.split(key, 2)
    base = jnp.clip(jax.random.normal(key_base, (PROMPTS, TOK_P, 3, HD), jnp.float32), -4.0, 4.0)
    row_scale = jnp.exp(jax.random.uniform(key_scale, (PROMPTS, TOK_P, 1, 1), jnp.float32, math.log(0.3), math.log(3.0)))
    which = jnp.arange(3).reshape(1, 1, 3, 1)
    base = jnp.where(which == 2, base * row_scale, base)
    return base.astype(jnp.bfloat16)


def draw_reveal_places(key, part):
    key = jax.random.fold_in(key, 23)
    segment_keys = jax.random.split(key, PROMPTS * SEGS_P)

    def pick(segment_key):
        return jax.random.permutation(segment_key, SEG)[:REV]
    chosen = jax.vmap(pick)(segment_keys)
    return chosen.reshape(PROMPTS, SEGS_P, REV).astype(jnp.int32)


def steps_of(own_key, extent, shards, low, top_value):
    def one(dim, blocks):
        draws = jax.random.uniform(jax.random.fold_in(jax.random.fold_in(own_key, 6), dim), (blocks,), jnp.float32, low / len(shards), top_value / len(shards))
        return jnp.repeat(jnp.exp(draws), extent[dim] // blocks).reshape((-1,) + (1,) * (len(extent) - dim - 1))

    factor_of = one(*shards[0])
    for cut in shards[1:]:
        factor_of = factor_of * one(*cut)
    return factor_of


def noise(key, dims, width, bound, cuts=(), kind=jnp.bfloat16):
    result = width * jax.random.normal(key, dims, jnp.float32)
    if cuts:
        result = result * steps_of(key, dims, cuts, -0.22, 0.18)
    return jnp.clip(result, -bound, bound).astype(kind)


def setup_inputs(seed: int = 0) -> dict:
    streams_of = jax.random.split(jax.random.key(seed), 5)
    answer_qkv = draw_answer_qkv(jax.random.fold_in(streams_of[4], 71), 0)
    prefix_kv = noise(streams_of[1], (PROMPTS, PREFIX, 2, HD), 1.0, 6.0, ((1, 4), (3, 32)))
    reveal_qkv = noise(streams_of[2], (PROMPTS, REVROWS, 3, HD), 1.0, 4.0, ((0, 4), (1, 32)))
    reveal_places = draw_reveal_places(jax.random.fold_in(streams_of[4], 71), 0)
    return {"answer_qkv": answer_qkv, "prefix_kv": prefix_kv, "reveal_qkv": reveal_qkv, "reveal_places": reveal_places}


def softmax_rows(queries, key_rows, value_rows):

    def per_head(pieces):
        scores = jnp.dot(pieces[0], pieces[1].T, preferred_element_type=jnp.float32) * (1.0 / math.sqrt(HEAD_DIM))
        maxima = lax.optimization_barrier(jnp.max(scores, axis=1, keepdims=True))
        weights = jnp.exp(scores - maxima)
        totals = lax.optimization_barrier(jnp.sum(weights, axis=1, keepdims=True))
        summed = jnp.dot(weights.astype(jnp.bfloat16), pieces[2], preferred_element_type=jnp.float32)
        return (summed / totals).astype(jnp.bfloat16)
    return lax.map(per_head, (queries, key_rows, value_rows))

def heads_first(matrix):
    return matrix.reshape(matrix.shape[0], HEADS, HEAD_DIM).transpose(1, 0, 2)

def one_prompt(qkv, prefix):
    prefix_keys = heads_first(prefix[:, 0])
    prefix_values = heads_first(prefix[:, 1])
    samples = qkv.reshape(SAMPLES, ANS, 3, HD)

    def per_sample(sample_rows):
        key_rows = jnp.concatenate([prefix_keys, heads_first(sample_rows[:, 1])], axis=1)
        value_rows = jnp.concatenate([prefix_values, heads_first(sample_rows[:, 2])], axis=1)
        output = softmax_rows(heads_first(sample_rows[:, 0]), key_rows, value_rows)
        return output.transpose(1, 0, 2).reshape(ANS, HD)
    return lax.map(per_sample, samples).reshape(TOK_P, HD)

def reference(answer_qkv, prefix_kv, reveal_qkv, reveal_places):
    segment_starts = jnp.arange(SEGS_P, dtype=jnp.int32)[:, None] * SEG
    positions = (segment_starts[None] + reveal_places.astype(jnp.int32)).reshape(PROMPTS, REVROWS)
    firsts = []
    seconds = []
    for prompt_index in range(PROMPTS):
        second_qkv = answer_qkv[prompt_index].at[positions[prompt_index]].set(reveal_qkv[prompt_index])
        firsts.append(one_prompt(answer_qkv[prompt_index], prefix_kv[prompt_index]))
        seconds.append(one_prompt(second_qkv, prefix_kv[prompt_index]))
    return (jnp.stack(firsts), jnp.stack(seconds))
```

```python
import functools
import math

import jax
import jax.numpy as jnp
from jax import lax
from jax.experimental import pallas as pl
from jax.experimental.pallas import tpu as pltpu
from jax.sharding import PartitionSpec as P

HEAD_DIM = 128
ANS = 1024
SEG = 128
REV = 16
KEPT = SEG - REV
ROWS = SEG + REV
SEGS = ANS // SEG
QUERIES = SEGS * ROWS
PREFIX = 2048
CHUNK = 512
RATE = math.log2(math.e) / math.sqrt(HEAD_DIM)
LIMIT = 100.0
AUG = HEAD_DIM + 16
NT = (((1,), (1,)), ((), ()))
VMEM_LIMIT = 60 * 2**20
OLD = SEGS * KEPT
NEW = OLD + SEGS * REV
SCALES = AUG - 8
PREFIX_COST = 10_000_000_000


def scores_of(keys, queries):
    return lax.dot_general(keys, queries, NT, preferred_element_type=jnp.float32)


def fold_max(scores):
    return jnp.max(scores.reshape(-1, 8, scores.shape[1]), axis=0)


def weigh(scores, reference_row):
    return jnp.exp2((scores - reference_row) * RATE).astype(jnp.bfloat16)


def scores_kernel(qk_ref, kp_ref, vpt_ref, acc_ref, weights_ref, queries_ref):
    queries_ref[: SEGS * SEG] = qk_ref[:, 0, :SEG].reshape(SEGS * SEG, HEAD_DIM)
    queries_ref[SEGS * SEG :] = qk_ref[:, 0, SEG:].reshape(SEGS * REV, HEAD_DIM)

    def attend(common_ref_row, one_ref_row, two_ref_row, first_scores):
        queries = queries_ref[...]
        total = None
        common_max = None
        for start in range(0, PREFIX, CHUNK):
            scores = first_scores if start == 0 and first_scores is not None else scores_of(
                kp_ref[start : start + CHUNK], queries
            )
            folded = fold_max(scores)
            common_max = folded if common_max is None else jnp.maximum(common_max, folded)
            part = jnp.dot(
                vpt_ref[:, start : start + CHUNK],
                weigh(scores, common_ref_row),
                preferred_element_type=jnp.float32,
            )
            total = part if total is None else total + part
        acc_ref[0] = total
        for start in range(0, SEGS, 2):
            keys = qk_ref[start : start + 2, 1, :KEPT].reshape(2 * KEPT, HEAD_DIM)
            scores = scores_of(keys, queries)
            common_max = jnp.maximum(common_max, fold_max(scores))
            weights_ref[0, start * KEPT : (start + 2) * KEPT] = weigh(scores, common_ref_row)
        old_scores = scores_of(qk_ref[:, 1, KEPT:SEG].reshape(SEGS * REV, HEAD_DIM), queries)
        weights_ref[0, OLD:NEW] = weigh(old_scores, one_ref_row)
        new_scores = scores_of(qk_ref[:, 1, SEG:].reshape(SEGS * REV, HEAD_DIM), queries)
        weights_ref[0, NEW:] = weigh(new_scores, two_ref_row)
        return common_max, fold_max(old_scores), fold_max(new_scores)

    first = scores_of(kp_ref[:CHUNK], queries_ref[...])
    start_row = jnp.max(first, axis=0, keepdims=True)
    common_max, old_max, new_max = attend(start_row, start_row, start_row, first)
    acc_ref[0, SCALES:] = jnp.ones((8, QUERIES), jnp.float32)
    largest = jnp.maximum(common_max, jnp.maximum(old_max, new_max))
    excess = jnp.max(largest - start_row) * RATE

    @pl.when(excess > LIMIT)
    def _():
        common_row = jnp.max(common_max, axis=0, keepdims=True)
        one_row = jnp.maximum(common_row, jnp.max(old_max, axis=0, keepdims=True))
        two_row = jnp.maximum(common_row, jnp.max(new_max, axis=0, keepdims=True))
        attend(common_row, one_row, two_row, None)
        acc_ref[0, SCALES : SCALES + 1] = jnp.exp2((common_row - one_row) * RATE)
        acc_ref[0, SCALES + 1 : SCALES + 2] = jnp.exp2((common_row - two_row) * RATE)


def attend_scores(qk, prefix_keys, prefix_values):
    samples = qk.shape[0] // SEGS
    whole = lambda i: (0, 0)
    per = lambda i: (i, 0, 0)
    return pl.pallas_call(
        scores_kernel,
        grid=(samples,),
        in_specs=[
            pl.BlockSpec((SEGS, 2, ROWS, HEAD_DIM), lambda i: (i, 0, 0, 0)),
            pl.BlockSpec((PREFIX, HEAD_DIM), whole),
            pl.BlockSpec((AUG, PREFIX), whole),
        ],
        out_specs=[
            pl.BlockSpec((1, AUG, QUERIES), per),
            pl.BlockSpec((1, QUERIES, QUERIES), per),
        ],
        out_shape=[
            jax.ShapeDtypeStruct((samples, AUG, QUERIES), jnp.float32),
            jax.ShapeDtypeStruct((samples, QUERIES, QUERIES), jnp.bfloat16),
        ],
        scratch_shapes=[pltpu.VMEM((QUERIES, HEAD_DIM), jnp.bfloat16)],
        compiler_params=pltpu.CompilerParams(vmem_limit_bytes=VMEM_LIMIT),
        cost_estimate=pl.CostEstimate(
            flops=12_000_000_000, bytes_accessed=20_000_000, transcendentals=15_000_000
        ),
        name="scores",
    )(qk, prefix_keys, prefix_values)


def values_kernel(v_ref, acc_ref, weights_ref, out_ref):
    def turned(rows):
        count = rows.shape[0]
        return jnp.concatenate([rows.T, jnp.ones((AUG - HEAD_DIM, count), jnp.bfloat16)], axis=0)

    def weighted(rows, weights):
        return jnp.dot(turned(rows), weights, preferred_element_type=jnp.float32)

    scale_one = acc_ref[0, SCALES : SCALES + 1]
    scale_two = acc_ref[0, SCALES + 1 : SCALES + 2]
    common = acc_ref[0] + weighted(
        v_ref[:, :KEPT].reshape(SEGS * KEPT, HEAD_DIM), weights_ref[0, :OLD]
    )
    one = common * scale_one + weighted(
        v_ref[:, KEPT:SEG].reshape(SEGS * REV, HEAD_DIM), weights_ref[0, OLD:NEW]
    )
    two = common * scale_two + weighted(
        v_ref[:, SEG:].reshape(SEGS * REV, HEAD_DIM), weights_ref[0, NEW:]
    )
    one = one[:HEAD_DIM] * (1.0 / one[HEAD_DIM : HEAD_DIM + 1])
    two = two[:HEAD_DIM] * (1.0 / two[HEAD_DIM : HEAD_DIM + 1])
    renewed = two[:, SEGS * SEG :]
    lane = lax.broadcasted_iota(jnp.int32, (HEAD_DIM, SEG), 1)
    for seg in range(SEGS):
        lanes = slice(seg * SEG, (seg + 1) * SEG)
        out_ref[seg, 0] = one[:, lanes].astype(jnp.bfloat16)
        shift = (KEPT - seg * REV) % SEG
        moved = pltpu.roll(renewed, shift, 1) if shift else renewed
        out_ref[seg, 1] = jnp.where(lane < KEPT, two[:, lanes], moved).astype(jnp.bfloat16)


def attend_values(values, acc, weights):
    samples = values.shape[0] // SEGS
    per = lambda i: (i, 0, 0)
    return pl.pallas_call(
        values_kernel,
        grid=(samples,),
        in_specs=[
            pl.BlockSpec((SEGS, ROWS, HEAD_DIM), per),
            pl.BlockSpec((1, AUG, QUERIES), per),
            pl.BlockSpec((1, QUERIES, QUERIES), per),
        ],
        out_specs=pl.BlockSpec((SEGS, 2, HEAD_DIM, SEG), lambda i: (i, 0, 0, 0)),
        out_shape=jax.ShapeDtypeStruct((samples * SEGS, 2, HEAD_DIM, SEG), jnp.bfloat16),
        compiler_params=pltpu.CompilerParams(vmem_limit_bytes=VMEM_LIMIT),
        name="values",
    )(values, acc, weights)


def place_kernel(heads, turned_ref, select_ref, one_ref, two_ref):
    for step, ref in enumerate((one_ref, two_ref)):
        ref[0] = lax.dot_general(
            select_ref[...],
            turned_ref[:, step].reshape(heads * HEAD_DIM, SEG),
            NT,
            preferred_element_type=jnp.float32,
        ).astype(jnp.bfloat16)


def place_outputs(turned, select):
    heads = 8
    count = turned.shape[0]
    shape = jax.ShapeDtypeStruct((1, SEG, count * HEAD_DIM), jnp.bfloat16)
    spec = pl.BlockSpec((1, SEG, heads * HEAD_DIM), lambda i: (0, 0, i))
    return pl.pallas_call(
        functools.partial(place_kernel, heads),
        grid=(count // heads,),
        in_specs=[
            pl.BlockSpec((heads, 2, HEAD_DIM, SEG), lambda i: (i, 0, 0, 0)),
            pl.BlockSpec((SEG, SEG), lambda i: (0, 0)),
        ],
        out_specs=[spec, spec],
        out_shape=[shape, shape],
        compiler_params=pltpu.CompilerParams(vmem_limit_bytes=VMEM_LIMIT),
        name="place",
    )(turned, select)


def row_order(places):
    rows = lax.broadcasted_iota(jnp.int32, (REV, SEG), 1)
    hits = jnp.where(places == rows, 1, 0)
    below = jnp.where(places < rows, 1, 0)
    rank = rows[:1] - jnp.sum(below, axis=0, keepdims=True)
    rank = jnp.where(jnp.sum(hits, axis=0, keepdims=True) > 0, -1, rank)
    kept = jnp.where(lax.broadcasted_iota(jnp.int32, (KEPT, SEG), 0) == rank, 1, 0)
    return jnp.concatenate([kept, hits], axis=0).astype(jnp.float32)


def pack_kernel(heads, kinds, places_ref, rows_ref, reveal_ref, out_ref, *rest):
    select = row_order(places_ref[...])
    if rest:
        rest[0][...] = select.T.astype(jnp.bfloat16)
    select = select.astype(jnp.bfloat16)
    for kind in range(kinds):
        moved = jnp.dot(select, rows_ref[0, kind], preferred_element_type=jnp.float32)
        moved = moved.astype(jnp.bfloat16)
        for head in range(heads):
            lanes = slice(head * HEAD_DIM, (head + 1) * HEAD_DIM)
            out_ref[head, kind, :SEG] = moved[:, lanes]
            out_ref[head, kind, SEG:] = reveal_ref[0, kind, :, lanes]


def pack(places, rows, reveal, first, kinds, with_select):
    heads = 8
    count = rows.shape[3] // HEAD_DIM
    width = heads * HEAD_DIM
    out_specs = [pl.BlockSpec((heads, kinds, ROWS, HEAD_DIM), lambda i: (i, 0, 0, 0))]
    out_shape = [jax.ShapeDtypeStruct((count, kinds, ROWS, HEAD_DIM), jnp.bfloat16)]
    if with_select:
        out_specs.append(pl.BlockSpec((SEG, SEG), lambda i: (0, 0)))
        out_shape.append(jax.ShapeDtypeStruct((SEG, SEG), jnp.bfloat16))
    return pl.pallas_call(
        functools.partial(pack_kernel, heads, kinds),
        grid=(count // heads,),
        in_specs=[
            pl.BlockSpec((REV, 1), lambda i: (0, 0)),
            pl.BlockSpec((1, kinds, SEG, width), lambda i: (0, first // kinds, 0, i)),
            pl.BlockSpec((1, kinds, REV, width), lambda i: (0, first // kinds, 0, i)),
        ],
        out_specs=out_specs,
        out_shape=out_shape,
        compiler_params=pltpu.CompilerParams(vmem_limit_bytes=VMEM_LIMIT),
        name="pack",
    )(places, rows, reveal)


def prefix_kernel(*refs):
    *parts, keys_ref, values_ref = refs
    values_ref[HEAD_DIM:] = jnp.ones((AUG - HEAD_DIM, PREFIX), jnp.bfloat16)
    for index, part in enumerate(parts):
        count = part.shape[1]
        span = slice(index * count, (index + 1) * count)
        keys_ref[span] = part[0]
        values_ref[:HEAD_DIM, span] = part[1].T


def arrange_prefix(parts):
    return pl.pallas_call(
        prefix_kernel,
        out_shape=[
            jax.ShapeDtypeStruct((PREFIX, HEAD_DIM), jnp.bfloat16),
            jax.ShapeDtypeStruct((AUG, PREFIX), jnp.bfloat16),
        ],
        compiler_params=pltpu.CompilerParams(vmem_limit_bytes=VMEM_LIMIT),
        cost_estimate=pl.CostEstimate(
            flops=PREFIX_COST, bytes_accessed=2_000_000, transcendentals=0
        ),
        name="prefix",
    )(*parts)


def exchange(array):
    return lax.all_to_all(array, "sample", split_axis=0, concat_axis=0, tiled=True)


def gather_prefix(prefix_kv):
    me = lax.axis_index("prompt")
    split = prefix_kv.transpose(0, 2, 1, 3)
    parts = []
    for flip in (3, 2, 1):
        pairs = [(i, i ^ flip) for i in range(4)]
        block = lax.dynamic_index_in_dim(split, me ^ flip, 0, keepdims=False)
        parts.append(lax.ppermute(block, "prompt", pairs))
    parts.append(lax.dynamic_index_in_dim(split, me, 0, keepdims=False))
    return parts


def local(answer_qkv, prefix_kv, reveal_qkv, reveal_places):
    places = reveal_places.reshape(REV, 1)
    rows = answer_qkv.transpose(0, 2, 1, 3)
    reveal = reveal_qkv.transpose(0, 2, 1, 3)
    parts = gather_prefix(prefix_kv)
    queries_keys = exchange(pack(places, rows, reveal, 0, 2, False)[0])
    late, select = pack(places, rows, reveal, 2, 1, True)
    prefix_keys, prefix_values = arrange_prefix(parts)
    late, queries_keys, prefix_keys, prefix_values = lax.optimization_barrier(
        (late, queries_keys, prefix_keys, prefix_values)
    )
    values = exchange(late)[:, 0]
    partial_results = attend_scores(queries_keys, prefix_keys, prefix_values)
    turned = exchange(attend_values(values, *partial_results))
    return place_outputs(turned, select)


def solution(mesh):
    placed = (
        P("prompt", "sample", None, None),
        P(None, "prompt", None, "sample"),
        P("prompt", "sample", None, None),
        P("prompt", "sample", None),
    )
    return jax.shard_map(
        local,
        mesh=mesh,
        in_specs=placed,
        out_specs=(P("prompt", "sample", None), P("prompt", "sample", None)),
        check_vma=False,
    )
```

```python
import functools
import math

import jax
import jax.numpy as jnp
from jax import lax
from jax.experimental import pallas as pl
from jax.experimental.pallas import tpu as pltpu
from jax.sharding import PartitionSpec as P

HEAD_DIM = 128
ANS = 1024
SEG = 128
REV = 16
KEPT = SEG - REV
ROWS = SEG + REV
SEGS = ANS // SEG
QUERIES = SEGS * ROWS
PREFIX = 2048
CHUNK = 512
RATE = math.log2(math.e) / math.sqrt(HEAD_DIM)
LIMIT = 100.0
AUG = HEAD_DIM + 16
NT = (((1,), (1,)), ((), ()))
FLIPS = (3, 2, 1)
VMEM_LIMIT = 63 * 2**20
FIRST = 128
SPAN = 4
PREFIX_COST = 60_000_000_000


def scores_of(keys, queries):
    return lax.dot_general(keys, queries, NT, preferred_element_type=jnp.float32)


def fold_max(scores):
    return jnp.max(scores.reshape(-1, 8, scores.shape[1]), axis=0)


def weigh(scores, reference_row):
    return jnp.exp2((scores - reference_row) * RATE).astype(jnp.bfloat16)


def attend_kernel(qkv_ref, kp_ref, vpt_ref, out_ref, queries_ref):
    queries_ref[: SEGS * SEG] = qkv_ref[:, 0, :SEG].reshape(SEGS * SEG, HEAD_DIM)
    queries_ref[SEGS * SEG :] = qkv_ref[:, 0, SEG:].reshape(SEGS * REV, HEAD_DIM)

    def answer_rows(kind, segs, rows):
        picked = qkv_ref[segs, kind, rows]
        return picked.reshape(picked.shape[0] * picked.shape[1], HEAD_DIM)

    def weighted(values, weights):
        ones = jnp.ones((AUG - HEAD_DIM, values.shape[0]), jnp.bfloat16)
        turned = jnp.concatenate([values.T, ones], axis=0)
        return jnp.dot(turned, weights, preferred_element_type=jnp.float32)

    def attend(common_row, one_row, two_row, scale_one, scale_two):
        queries = queries_ref[...]
        total = None
        common_max = None
        for start in range(0, PREFIX, CHUNK):
            scores = scores_of(kp_ref[start : start + CHUNK], queries)
            folded = fold_max(scores)
            common_max = folded if common_max is None else jnp.maximum(common_max, folded)
            part = jnp.dot(
                vpt_ref[:, start : start + CHUNK],
                weigh(scores, common_row),
                preferred_element_type=jnp.float32,
            )
            total = part if total is None else total + part
        for start in range(0, SEGS, SPAN):
            segs = slice(start, start + SPAN)
            scores = scores_of(answer_rows(1, segs, slice(0, KEPT)), queries)
            common_max = jnp.maximum(common_max, fold_max(scores))
            total += weighted(answer_rows(2, segs, slice(0, KEPT)), weigh(scores, common_row))

        def step(rows, row, scale):
            scores = scores_of(answer_rows(1, slice(0, SEGS), rows), queries)
            own = weighted(answer_rows(2, slice(0, SEGS), rows), weigh(scores, row))
            own += total if scale is None else total * scale
            return own[:HEAD_DIM] * (1.0 / own[HEAD_DIM : HEAD_DIM + 1]), fold_max(scores)

        one, one_max = step(slice(KEPT, SEG), one_row, scale_one)
        two, two_max = step(slice(SEG, ROWS), two_row, scale_two)
        renewed = two[:, SEGS * SEG :]
        lane = lax.broadcasted_iota(jnp.int32, (HEAD_DIM, SEG), 1)
        for seg in range(SEGS):
            lanes = slice(seg * SEG, (seg + 1) * SEG)
            out_ref[seg, 0] = one[:, lanes].astype(jnp.bfloat16)
            shift = (KEPT - seg * REV) % SEG
            moved = pltpu.roll(renewed, shift, 1) if shift else renewed
            out_ref[seg, 1] = jnp.where(lane < KEPT, two[:, lanes], moved).astype(jnp.bfloat16)
        return common_max, one_max, two_max

    first = scores_of(kp_ref[:FIRST], queries_ref[...])
    start_row = jnp.max(first, axis=0, keepdims=True)
    common_max, one_max, two_max = attend(start_row, start_row, start_row, None, None)
    largest = jnp.maximum(common_max, jnp.maximum(one_max, two_max))
    excess = jnp.max(largest - start_row) * RATE

    @pl.when(excess > LIMIT)
    def _():
        common_row = jnp.max(common_max, axis=0, keepdims=True)
        one_row = jnp.maximum(common_row, jnp.max(one_max, axis=0, keepdims=True))
        two_row = jnp.maximum(common_row, jnp.max(two_max, axis=0, keepdims=True))
        attend(
            common_row,
            one_row,
            two_row,
            jnp.exp2((common_row - one_row) * RATE),
            jnp.exp2((common_row - two_row) * RATE),
        )


def attend(qkv, prefix_keys, prefix_values):
    samples = qkv.shape[0] // SEGS
    whole = lambda i: (0, 0)
    per = lambda i: (i, 0, 0, 0)
    return pl.pallas_call(
        attend_kernel,
        grid=(samples,),
        in_specs=[
            pl.BlockSpec((SEGS, 3, ROWS, HEAD_DIM), per),
            pl.BlockSpec((PREFIX, HEAD_DIM), whole),
            pl.BlockSpec((AUG, PREFIX), whole),
        ],
        out_specs=pl.BlockSpec((SEGS, 2, HEAD_DIM, SEG), per),
        out_shape=jax.ShapeDtypeStruct((samples * SEGS, 2, HEAD_DIM, SEG), jnp.bfloat16),
        scratch_shapes=[pltpu.VMEM((QUERIES, HEAD_DIM), jnp.bfloat16)],
        compiler_params=pltpu.CompilerParams(vmem_limit_bytes=VMEM_LIMIT),
        cost_estimate=pl.CostEstimate(
            flops=14_000_000_000, bytes_accessed=7_000_000, transcendentals=15_000_000
        ),
        name="attend",
    )(qkv, prefix_keys, prefix_values)


def place_kernel(heads, turned_ref, select_ref, one_ref, two_ref):
    for step, ref in enumerate((one_ref, two_ref)):
        ref[0] = lax.dot_general(
            select_ref[...],
            turned_ref[:, step].reshape(heads * HEAD_DIM, SEG),
            NT,
            preferred_element_type=jnp.float32,
        ).astype(jnp.bfloat16)


def place_outputs(turned, select):
    heads = 16
    count = turned.shape[0]
    shape = jax.ShapeDtypeStruct((1, SEG, count * HEAD_DIM), jnp.bfloat16)
    spec = pl.BlockSpec((1, SEG, heads * HEAD_DIM), lambda i: (0, 0, i))
    return pl.pallas_call(
        functools.partial(place_kernel, heads),
        grid=(count // heads,),
        in_specs=[
            pl.BlockSpec((heads, 2, HEAD_DIM, SEG), lambda i: (i, 0, 0, 0)),
            pl.BlockSpec((SEG, SEG), lambda i: (0, 0)),
        ],
        out_specs=[spec, spec],
        out_shape=[shape, shape],
        compiler_params=pltpu.CompilerParams(vmem_limit_bytes=VMEM_LIMIT),
        name="place",
    )(turned, select)


def row_order(places):
    diagonal = lax.broadcasted_iota(jnp.int32, (REV, REV), 0) == lax.broadcasted_iota(
        jnp.int32, (REV, REV), 1
    )
    column = jnp.sum(jnp.where(diagonal, places, 0), axis=1, keepdims=True)
    rows = lax.broadcasted_iota(jnp.int32, (REV, SEG), 1)
    hits = jnp.where(column == rows, 1, 0)
    below = jnp.where(column < rows, 1, 0)
    rank = rows[:1] - jnp.sum(below, axis=0, keepdims=True)
    rank = jnp.where(jnp.sum(hits, axis=0, keepdims=True) > 0, -1, rank)
    kept = jnp.where(lax.broadcasted_iota(jnp.int32, (KEPT, SEG), 0) == rank, 1, 0)
    return jnp.concatenate([kept, hits], axis=0).astype(jnp.float32)


def prefix_copies(prefix_ref, part_refs, sems):
    me = lax.axis_index("prompt")
    return [
        pltpu.make_async_copy(prefix_ref.at[me ^ flip], ref, sems.at[index])
        for index, (flip, ref) in enumerate(zip(FLIPS, part_refs))
    ]


def pack_kernel(
    heads, places_ref, rows_ref, reveal_ref, prefix_ref, out_ref, select_ref, *rest
):
    *part_refs, order_ref, sems = rest
    copies = prefix_copies(prefix_ref, part_refs, sems)

    @pl.when(pl.program_id(0) == 0)
    def _():
        for copy in copies:
            copy.start()
        order = row_order(places_ref[...])
        order_ref[...] = order.astype(jnp.bfloat16)
        select_ref[...] = order.T.astype(jnp.bfloat16)

    for kind in range(3):
        moved = jnp.dot(order_ref[...], rows_ref[0, kind], preferred_element_type=jnp.float32)
        moved = moved.astype(jnp.bfloat16)
        for head in range(heads):
            lanes = slice(head * HEAD_DIM, (head + 1) * HEAD_DIM)
            out_ref[head, kind, :SEG] = moved[:, lanes]
            out_ref[head, kind, SEG:] = reveal_ref[0, kind, :, lanes]

    @pl.when(pl.program_id(0) == pl.num_programs(0) - 1)
    def _():
        for copy in copies:
            copy.wait()


def pack(places, rows, reveal, prefix):
    heads = 16
    count = rows.shape[3] // HEAD_DIM
    width = heads * HEAD_DIM
    part = jax.ShapeDtypeStruct(prefix.shape[1:], jnp.bfloat16)
    return pl.pallas_call(
        functools.partial(pack_kernel, heads),
        grid=(count // heads,),
        in_specs=[
            pl.BlockSpec((1, REV), lambda i: (0, 0)),
            pl.BlockSpec((1, 3, SEG, width), lambda i: (0, 0, 0, i)),
            pl.BlockSpec((1, 3, REV, width), lambda i: (0, 0, 0, i)),
            pl.BlockSpec(memory_space=pl.ANY),
        ],
        out_specs=[
            pl.BlockSpec((heads, 3, ROWS, HEAD_DIM), lambda i: (i, 0, 0, 0)),
            pl.BlockSpec((SEG, SEG), lambda i: (0, 0)),
        ]
        + [pl.BlockSpec(part.shape, lambda i: (0, 0, 0))] * len(FLIPS),
        out_shape=[
            jax.ShapeDtypeStruct((count, 3, ROWS, HEAD_DIM), jnp.bfloat16),
            jax.ShapeDtypeStruct((SEG, SEG), jnp.bfloat16),
        ]
        + [part] * len(FLIPS),
        scratch_shapes=[
            pltpu.VMEM((SEG, SEG), jnp.bfloat16),
            pltpu.SemaphoreType.DMA((len(FLIPS),)),
        ],
        compiler_params=pltpu.CompilerParams(vmem_limit_bytes=VMEM_LIMIT),
        name="pack",
    )(places, rows, reveal, prefix)


def prefix_kernel(*refs):
    *parts, prefix_ref, keys_ref, values_ref, own_ref, sem = refs
    copy = pltpu.make_async_copy(prefix_ref.at[lax.axis_index("prompt")], own_ref, sem)
    copy.start()
    values_ref[HEAD_DIM:] = jnp.ones((AUG - HEAD_DIM, PREFIX), jnp.bfloat16)
    count = own_ref.shape[0]
    for index, part in enumerate((*parts, own_ref)):
        if part is own_ref:
            copy.wait()
        span = slice(index * count, (index + 1) * count)
        keys_ref[span] = part[:, 0]
        values_ref[:HEAD_DIM, span] = part[:, 1].T


def arrange_prefix(parts, prefix):
    vmem = pl.BlockSpec(memory_space=pltpu.VMEM)
    return pl.pallas_call(
        prefix_kernel,
        in_specs=[vmem] * len(parts) + [pl.BlockSpec(memory_space=pl.ANY)],
        out_specs=[vmem] * 2,
        out_shape=[
            jax.ShapeDtypeStruct((PREFIX, HEAD_DIM), jnp.bfloat16),
            jax.ShapeDtypeStruct((AUG, PREFIX), jnp.bfloat16),
        ],
        scratch_shapes=[
            pltpu.VMEM(prefix.shape[1:], jnp.bfloat16),
            pltpu.SemaphoreType.DMA,
        ],
        compiler_params=pltpu.CompilerParams(vmem_limit_bytes=VMEM_LIMIT),
        cost_estimate=pl.CostEstimate(
            flops=PREFIX_COST, bytes_accessed=2_000_000, transcendentals=0
        ),
        name="prefix",
    )(*parts, prefix)


def exchange(array):
    return lax.all_to_all(array, "sample", split_axis=0, concat_axis=0, tiled=True)


def trade(part, flip):
    return lax.ppermute(part, "prompt", [(i, i ^ flip) for i in range(4)])


def local(answer_qkv, prefix_kv, reveal_qkv, reveal_places):
    packed, select, *parts = pack(
        reveal_places.reshape(1, REV),
        answer_qkv.transpose(0, 2, 1, 3),
        reveal_qkv.transpose(0, 2, 1, 3),
        prefix_kv,
    )
    parts = [trade(part, flip) for part, flip in zip(parts, FLIPS)]
    grouped = exchange(packed)
    turned = exchange(attend(grouped, *arrange_prefix(parts, prefix_kv)))
    return place_outputs(turned, select)


def solution(mesh):
    placed = (
        P("prompt", "sample", None, None),
        P(None, "prompt", None, "sample"),
        P("prompt", "sample", None, None),
        P("prompt", "sample", None),
    )
    return jax.shard_map(
        local,
        mesh=mesh,
        in_specs=placed,
        out_specs=(P("prompt", "sample", None), P("prompt", "sample", None)),
        check_vma=False,
    )
```

```python
import functools
import math

import jax
import jax.numpy as jnp
from jax import lax
from jax.experimental import pallas as pl
from jax.experimental.pallas import tpu as pltpu
from jax.sharding import PartitionSpec as P

HEAD_DIM = 128
ANS = 1024
SEG = 128
REV = 16
KEPT = SEG - REV
ROWS = SEG + REV
SEGS = ANS // SEG
QUERIES = SEGS * ROWS
PREFIX = 2048
CHUNK = 512
RATE = math.log2(math.e) / math.sqrt(HEAD_DIM)
LIMIT = 100.0
AUG = HEAD_DIM + 16
NT = (((1,), (1,)), ((), ()))
FLIPS = (3, 2, 1)
VMEM_LIMIT = 63 * 2**20
FIRST = 128
SPAN = 4
GROUP = 2
PLACE_LIMIT = 20 * 2**20
PREFIX_COST = 60_000_000_000


def scores_of(keys, queries):
    return lax.dot_general(keys, queries, NT, preferred_element_type=jnp.float32)


def fold_max(scores):
    return jnp.max(scores.reshape(-1, 8, scores.shape[1]), axis=0)


def weigh(scores, reference_row):
    return jnp.exp2((scores - reference_row) * RATE).astype(jnp.bfloat16)


def attend_kernel(group, qkv_ref, kp_ref, vpt_ref, out_ref, queries_ref, total_ref):
    for sample in range(group):
        segs = slice(sample * SEGS, (sample + 1) * SEGS)
        at = sample * QUERIES
        queries_ref[at : at + SEGS * SEG] = qkv_ref[segs, 0, :SEG].reshape(-1, HEAD_DIM)
        queries_ref[at + SEGS * SEG : at + QUERIES] = qkv_ref[segs, 0, SEG:].reshape(-1, HEAD_DIM)

    def weighted(values, weights):
        ones = jnp.ones((AUG - HEAD_DIM, values.shape[0]), jnp.bfloat16)
        turned = jnp.concatenate([values.T, ones], axis=0)
        return jnp.dot(turned, weights, preferred_element_type=jnp.float32)

    def answer_rows(kind, first_seg, segs, rows):
        return qkv_ref[first_seg : first_seg + segs, kind, rows].reshape(-1, HEAD_DIM)

    def step(sample, total, rows, row):
        queries = queries_ref[sample * QUERIES : (sample + 1) * QUERIES]
        scores = scores_of(answer_rows(1, sample * SEGS, SEGS, rows), queries)
        own = weighted(answer_rows(2, sample * SEGS, SEGS, rows), weigh(scores, row)) + total
        return own[:HEAD_DIM] * (1.0 / own[HEAD_DIM : HEAD_DIM + 1]), fold_max(scores)

    def store(sample, one, two):
        renewed = two[:, SEGS * SEG :]
        lane = lax.broadcasted_iota(jnp.int32, (HEAD_DIM, SEG), 1)
        for seg in range(SEGS):
            lanes = slice(seg * SEG, (seg + 1) * SEG)
            out_ref[sample * SEGS + seg, 0] = one[:, lanes].astype(jnp.bfloat16)
            shift = (KEPT - seg * REV) % SEG
            moved = pltpu.roll(renewed, shift, 1) if shift else renewed
            merged = jnp.where(lane < KEPT, two[:, lanes], moved)
            out_ref[sample * SEGS + seg, 1] = merged.astype(jnp.bfloat16)

    queries = queries_ref[...]
    start_row = jnp.max(scores_of(kp_ref[:FIRST], queries), axis=0, keepdims=True)
    prefix_total = None
    prefix_max = None
    for start in range(0, PREFIX, CHUNK):
        scores = scores_of(kp_ref[start : start + CHUNK], queries)
        folded = fold_max(scores)
        prefix_max = folded if prefix_max is None else jnp.maximum(prefix_max, folded)
        part = jnp.dot(
            vpt_ref[:, start : start + CHUNK],
            weigh(scores, start_row),
            preferred_element_type=jnp.float32,
        )
        prefix_total = part if prefix_total is None else prefix_total + part

    largest = []
    excess = None
    for sample in range(group):
        lanes = slice(sample * QUERIES, (sample + 1) * QUERIES)
        row = start_row[:, lanes]
        total = prefix_total[:, lanes]
        common_max = prefix_max[:, lanes]
        for start in range(0, SEGS, SPAN):
            first_seg = sample * SEGS + start
            scores = scores_of(answer_rows(1, first_seg, SPAN, slice(0, KEPT)), queries[lanes])
            common_max = jnp.maximum(common_max, fold_max(scores))
            total += weighted(
                answer_rows(2, first_seg, SPAN, slice(0, KEPT)), weigh(scores, row)
            )
        one, one_max = step(sample, total, slice(KEPT, SEG), row)
        two, two_max = step(sample, total, slice(SEG, ROWS), row)
        store(sample, one, two)
        largest.append((common_max, one_max, two_max))
        above = jnp.maximum(common_max, jnp.maximum(one_max, two_max)) - row
        excess = above if excess is None else jnp.maximum(excess, above)

    @pl.when(jnp.max(excess) * RATE > LIMIT)
    def _():
        for sample, (common_max, one_max, two_max) in enumerate(largest):
            rows = slice(sample * QUERIES, (sample + 1) * QUERIES)
            common_row = jnp.max(common_max, axis=0, keepdims=True)
            one_row = jnp.maximum(common_row, jnp.max(one_max, axis=0, keepdims=True))
            two_row = jnp.maximum(common_row, jnp.max(two_max, axis=0, keepdims=True))
            total_ref[...] = jnp.zeros_like(total_ref)

            def add_prefix(index, carry):
                span = pl.ds(pl.multiple_of(index * FIRST, FIRST), FIRST)
                weights = weigh(scores_of(kp_ref[span], queries_ref[rows]), common_row)
                total_ref[...] += jnp.dot(
                    vpt_ref[:, span], weights, preferred_element_type=jnp.float32
                )
                return carry

            def add_answers(seg, carry):
                scores = scores_of(qkv_ref[seg, 1, :KEPT], queries_ref[rows])
                total_ref[...] += weighted(qkv_ref[seg, 2, :KEPT], weigh(scores, common_row))
                return carry

            lax.fori_loop(0, PREFIX // FIRST, add_prefix, 0)
            lax.fori_loop(sample * SEGS, (sample + 1) * SEGS, add_answers, 0)
            scale_one = jnp.exp2((common_row - one_row) * RATE)
            scale_two = jnp.exp2((common_row - two_row) * RATE)
            one, _ = step(sample, total_ref[...] * scale_one, slice(KEPT, SEG), one_row)
            two, _ = step(sample, total_ref[...] * scale_two, slice(SEG, ROWS), two_row)
            store(sample, one, two)


def attend(qkv, prefix_keys, prefix_values):
    samples = qkv.shape[0] // SEGS
    group = GROUP
    whole = lambda i: (0, 0)
    per = lambda i: (i, 0, 0, 0)
    return pl.pallas_call(
        functools.partial(attend_kernel, group),
        grid=(samples // group,),
        in_specs=[
            pl.BlockSpec((group * SEGS, 3, ROWS, HEAD_DIM), per),
            pl.BlockSpec((PREFIX, HEAD_DIM), whole),
            pl.BlockSpec((AUG, PREFIX), whole),
        ],
        out_specs=pl.BlockSpec((group * SEGS, 2, HEAD_DIM, SEG), per),
        out_shape=jax.ShapeDtypeStruct((samples * SEGS, 2, HEAD_DIM, SEG), jnp.bfloat16),
        scratch_shapes=[
            pltpu.VMEM((group * QUERIES, HEAD_DIM), jnp.bfloat16),
            pltpu.VMEM((AUG, QUERIES), jnp.float32),
        ],
        compiler_params=pltpu.CompilerParams(vmem_limit_bytes=VMEM_LIMIT),
        cost_estimate=pl.CostEstimate(
            flops=14_000_000_000, bytes_accessed=7_000_000, transcendentals=15_000_000
        ),
        name="attend",
    )(qkv, prefix_keys, prefix_values)


def place_kernel(heads, turned_ref, select_ref, one_ref, two_ref):
    for step, ref in enumerate((one_ref, two_ref)):
        ref[0] = lax.dot_general(
            select_ref[...],
            turned_ref[:, step].reshape(heads * HEAD_DIM, SEG),
            NT,
            preferred_element_type=jnp.float32,
        ).astype(jnp.bfloat16)


def place_outputs(turned, select):
    heads = 16
    count = turned.shape[0]
    shape = jax.ShapeDtypeStruct((1, SEG, count * HEAD_DIM), jnp.bfloat16)
    spec = pl.BlockSpec((1, SEG, heads * HEAD_DIM), lambda i: (0, 0, i))
    return pl.pallas_call(
        functools.partial(place_kernel, heads),
        grid=(count // heads,),
        in_specs=[
            pl.BlockSpec((heads, 2, HEAD_DIM, SEG), lambda i: (i, 0, 0, 0)),
            pl.BlockSpec((SEG, SEG), lambda i: (0, 0)),
        ],
        out_specs=[spec, spec],
        out_shape=[shape, shape],
        compiler_params=pltpu.CompilerParams(vmem_limit_bytes=PLACE_LIMIT),
        name="place",
    )(turned, select)


def row_order(places):
    diagonal = lax.broadcasted_iota(jnp.int32, (REV, REV), 0) == lax.broadcasted_iota(
        jnp.int32, (REV, REV), 1
    )
    column = jnp.sum(jnp.where(diagonal, places, 0), axis=1, keepdims=True)
    rows = lax.broadcasted_iota(jnp.int32, (REV, SEG), 1)
    hits = jnp.where(column == rows, 1, 0)
    below = jnp.where(column < rows, 1, 0)
    rank = rows[:1] - jnp.sum(below, axis=0, keepdims=True)
    rank = jnp.where(jnp.sum(hits, axis=0, keepdims=True) > 0, -1, rank)
    kept = jnp.where(lax.broadcasted_iota(jnp.int32, (KEPT, SEG), 0) == rank, 1, 0)
    return jnp.concatenate([kept, hits], axis=0).astype(jnp.float32)


def prefix_copies(prefix_ref, part_refs, sems):
    me = lax.axis_index("prompt")
    return [
        pltpu.make_async_copy(prefix_ref.at[me ^ flip], ref, sems.at[index])
        for index, (flip, ref) in enumerate(zip(FLIPS, part_refs))
    ]


def pack_kernel(
    heads, places_ref, rows_ref, reveal_ref, prefix_ref, out_ref, select_ref, *rest
):
    *part_refs, order_ref, sems = rest
    copies = prefix_copies(prefix_ref, part_refs, sems)

    @pl.when(pl.program_id(0) == 0)
    def _():
        for copy in copies:
            copy.start()
        order = row_order(places_ref[...])
        order_ref[...] = order.astype(jnp.bfloat16)
        select_ref[...] = order.T.astype(jnp.bfloat16)

    for kind in range(3):
        moved = jnp.dot(order_ref[...], rows_ref[0, kind], preferred_element_type=jnp.float32)
        moved = moved.astype(jnp.bfloat16)
        for head in range(heads):
            lanes = slice(head * HEAD_DIM, (head + 1) * HEAD_DIM)
            out_ref[head, kind, :SEG] = moved[:, lanes]
            out_ref[head, kind, SEG:] = reveal_ref[0, kind, :, lanes]

    @pl.when(pl.program_id(0) == pl.num_programs(0) - 1)
    def _():
        for copy in copies:
            copy.wait()


def pack(places, rows, reveal, prefix):
    heads = 16
    count = rows.shape[3] // HEAD_DIM
    width = heads * HEAD_DIM
    part = jax.ShapeDtypeStruct(prefix.shape[1:], jnp.bfloat16)
    return pl.pallas_call(
        functools.partial(pack_kernel, heads),
        grid=(count // heads,),
        in_specs=[
            pl.BlockSpec((1, REV), lambda i: (0, 0)),
            pl.BlockSpec((1, 3, SEG, width), lambda i: (0, 0, 0, i)),
            pl.BlockSpec((1, 3, REV, width), lambda i: (0, 0, 0, i)),
            pl.BlockSpec(memory_space=pl.ANY),
        ],
        out_specs=[
            pl.BlockSpec((heads, 3, ROWS, HEAD_DIM), lambda i: (i, 0, 0, 0)),
            pl.BlockSpec((SEG, SEG), lambda i: (0, 0)),
        ]
        + [pl.BlockSpec(part.shape, lambda i: (0, 0, 0))] * len(FLIPS),
        out_shape=[
            jax.ShapeDtypeStruct((count, 3, ROWS, HEAD_DIM), jnp.bfloat16),
            jax.ShapeDtypeStruct((SEG, SEG), jnp.bfloat16),
        ]
        + [part] * len(FLIPS),
        scratch_shapes=[
            pltpu.VMEM((SEG, SEG), jnp.bfloat16),
            pltpu.SemaphoreType.DMA((len(FLIPS),)),
        ],
        compiler_params=pltpu.CompilerParams(vmem_limit_bytes=VMEM_LIMIT),
        name="pack",
    )(places, rows, reveal, prefix)


def prefix_kernel(*refs):
    *parts, prefix_ref, keys_ref, values_ref, own_ref, sem = refs
    copy = pltpu.make_async_copy(prefix_ref.at[lax.axis_index("prompt")], own_ref, sem)
    copy.start()
    values_ref[HEAD_DIM:] = jnp.ones((AUG - HEAD_DIM, PREFIX), jnp.bfloat16)
    count = own_ref.shape[0]
    for index, part in enumerate((*parts, own_ref)):
        if part is own_ref:
            copy.wait()
        span = slice(index * count, (index + 1) * count)
        keys_ref[span] = part[:, 0]
        values_ref[:HEAD_DIM, span] = part[:, 1].T


def arrange_prefix(parts, prefix):
    vmem = pl.BlockSpec(memory_space=pltpu.VMEM)
    return pl.pallas_call(
        prefix_kernel,
        in_specs=[vmem] * len(parts) + [pl.BlockSpec(memory_space=pl.ANY)],
        out_specs=[vmem] * 2,
        out_shape=[
            jax.ShapeDtypeStruct((PREFIX, HEAD_DIM), jnp.bfloat16),
            jax.ShapeDtypeStruct((AUG, PREFIX), jnp.bfloat16),
        ],
        scratch_shapes=[
            pltpu.VMEM(prefix.shape[1:], jnp.bfloat16),
            pltpu.SemaphoreType.DMA,
        ],
        compiler_params=pltpu.CompilerParams(vmem_limit_bytes=VMEM_LIMIT),
        cost_estimate=pl.CostEstimate(
            flops=PREFIX_COST, bytes_accessed=2_000_000, transcendentals=0
        ),
        name="prefix",
    )(*parts, prefix)


def exchange(array):
    return lax.all_to_all(array, "sample", split_axis=0, concat_axis=0, tiled=True)


def trade(part, flip):
    return lax.ppermute(part, "prompt", [(i, i ^ flip) for i in range(4)])


def local(answer_qkv, prefix_kv, reveal_qkv, reveal_places):
    packed, select, *parts = pack(
        reveal_places.reshape(1, REV),
        answer_qkv.transpose(0, 2, 1, 3),
        reveal_qkv.transpose(0, 2, 1, 3),
        prefix_kv,
    )
    parts = [trade(part, flip) for part, flip in zip(parts, FLIPS)]
    grouped = exchange(packed)
    turned = exchange(attend(grouped, *arrange_prefix(parts, prefix_kv)))
    return place_outputs(turned, select)


def solution(mesh):
    placed = (
        P("prompt", "sample", None, None),
        P(None, "prompt", None, "sample"),
        P("prompt", "sample", None, None),
        P("prompt", "sample", None),
    )
    return jax.shard_map(
        local,
        mesh=mesh,
        in_specs=placed,
        out_specs=(P("prompt", "sample", None), P("prompt", "sample", None)),
        check_vma=False,
    )
```

```python
import functools
import math

import jax
import jax.numpy as jnp
from jax import lax
from jax.experimental import pallas as pl
from jax.experimental.pallas import tpu as pltpu
from jax.sharding import PartitionSpec as P

HEAD_DIM = 128
ANS = 1024
SEG = 128
REV = 16
KEPT = SEG - REV
ROWS = SEG + REV
SEGS = ANS // SEG
QUERIES = SEGS * ROWS
PREFIX = 2048
CHUNK = 512
RATE = math.log2(math.e) / math.sqrt(HEAD_DIM)
LIMIT = 100.0
AUG = HEAD_DIM + 16
NT = (((1,), (1,)), ((), ()))
FLIPS = (3, 2, 1)
VMEM_LIMIT = 63 * 2**20
FIRST = 128
SPAN = 4
GROUP = 2
PLACE_LIMIT = 20 * 2**20
ATTEND_LIMIT = 44 * 2**20
PREFIX_COST = 60_000_000_000


def scores_of(keys, queries):
    return lax.dot_general(keys, queries, NT, preferred_element_type=jnp.float32)


def fold_max(scores):
    return jnp.max(scores.reshape(-1, 8, scores.shape[1]), axis=0)


def weigh(scores, reference_row):
    return jnp.exp2((scores - reference_row) * RATE).astype(jnp.bfloat16)


def attend_kernel(group, qkv_ref, kp_ref, vpt_ref, out_ref, queries_ref, total_ref):
    for sample in range(group):
        segs = slice(sample * SEGS, (sample + 1) * SEGS)
        at = sample * QUERIES
        queries_ref[at : at + SEGS * SEG] = qkv_ref[segs, 0, :SEG].reshape(-1, HEAD_DIM)
        queries_ref[at + SEGS * SEG : at + QUERIES] = qkv_ref[segs, 0, SEG:].reshape(-1, HEAD_DIM)

    def weighted(values, weights):
        ones = jnp.ones((AUG - HEAD_DIM, values.shape[0]), jnp.bfloat16)
        turned = jnp.concatenate([values.T, ones], axis=0)
        return jnp.dot(turned, weights, preferred_element_type=jnp.float32)

    def answer_rows(kind, first_seg, segs, rows):
        return qkv_ref[first_seg : first_seg + segs, kind, rows].reshape(-1, HEAD_DIM)

    def step(sample, total, rows, row):
        queries = queries_ref[sample * QUERIES : (sample + 1) * QUERIES]
        scores = scores_of(answer_rows(1, sample * SEGS, SEGS, rows), queries)
        own = weighted(answer_rows(2, sample * SEGS, SEGS, rows), weigh(scores, row)) + total
        return own[:HEAD_DIM] * (1.0 / own[HEAD_DIM : HEAD_DIM + 1]), fold_max(scores)

    def store(sample, one, two):
        renewed = two[:, SEGS * SEG :]
        lane = lax.broadcasted_iota(jnp.int32, (HEAD_DIM, SEG), 1)
        for seg in range(SEGS):
            lanes = slice(seg * SEG, (seg + 1) * SEG)
            out_ref[sample * SEGS + seg, 0] = one[:, lanes].astype(jnp.bfloat16)
            shift = (KEPT - seg * REV) % SEG
            moved = pltpu.roll(renewed, shift, 1) if shift else renewed
            merged = jnp.where(lane < KEPT, two[:, lanes], moved)
            out_ref[sample * SEGS + seg, 1] = merged.astype(jnp.bfloat16)

    queries = queries_ref[...]
    start_row = jnp.max(scores_of(kp_ref[:FIRST], queries), axis=0, keepdims=True)
    prefix_total = None
    prefix_max = None
    for start in range(0, PREFIX, CHUNK):
        scores = scores_of(kp_ref[start : start + CHUNK], queries)
        folded = fold_max(scores)
        prefix_max = folded if prefix_max is None else jnp.maximum(prefix_max, folded)
        part = jnp.dot(
            vpt_ref[:, start : start + CHUNK],
            weigh(scores, start_row),
            preferred_element_type=jnp.float32,
        )
        prefix_total = part if prefix_total is None else prefix_total + part

    largest = []
    excess = None
    for sample in range(group):
        lanes = slice(sample * QUERIES, (sample + 1) * QUERIES)
        row = start_row[:, lanes]
        total = prefix_total[:, lanes]
        common_max = prefix_max[:, lanes]
        for start in range(0, SEGS, SPAN):
            first_seg = sample * SEGS + start
            scores = scores_of(answer_rows(1, first_seg, SPAN, slice(0, KEPT)), queries[lanes])
            common_max = jnp.maximum(common_max, fold_max(scores))
            total += weighted(
                answer_rows(2, first_seg, SPAN, slice(0, KEPT)), weigh(scores, row)
            )
        one, one_max = step(sample, total, slice(KEPT, SEG), row)
        two, two_max = step(sample, total, slice(SEG, ROWS), row)
        store(sample, one, two)
        largest.append((common_max, one_max, two_max))
        above = jnp.maximum(common_max, jnp.maximum(one_max, two_max)) - row
        excess = above if excess is None else jnp.maximum(excess, above)

    @pl.when(jnp.max(excess) * RATE > LIMIT)
    def _():
        for sample, (common_max, one_max, two_max) in enumerate(largest):
            rows = slice(sample * QUERIES, (sample + 1) * QUERIES)
            common_row = jnp.max(common_max, axis=0, keepdims=True)
            one_row = jnp.maximum(common_row, jnp.max(one_max, axis=0, keepdims=True))
            two_row = jnp.maximum(common_row, jnp.max(two_max, axis=0, keepdims=True))
            total_ref[...] = jnp.zeros_like(total_ref)

            def add_prefix(index, carry):
                span = pl.ds(pl.multiple_of(index * FIRST, FIRST), FIRST)
                weights = weigh(scores_of(kp_ref[span], queries_ref[rows]), common_row)
                total_ref[...] += jnp.dot(
                    vpt_ref[:, span], weights, preferred_element_type=jnp.float32
                )
                return carry

            def add_answers(seg, carry):
                scores = scores_of(qkv_ref[seg, 1, :KEPT], queries_ref[rows])
                total_ref[...] += weighted(qkv_ref[seg, 2, :KEPT], weigh(scores, common_row))
                return carry

            lax.fori_loop(0, PREFIX // FIRST, add_prefix, 0)
            lax.fori_loop(sample * SEGS, (sample + 1) * SEGS, add_answers, 0)
            scale_one = jnp.exp2((common_row - one_row) * RATE)
            scale_two = jnp.exp2((common_row - two_row) * RATE)
            one, _ = step(sample, total_ref[...] * scale_one, slice(KEPT, SEG), one_row)
            two, _ = step(sample, total_ref[...] * scale_two, slice(SEG, ROWS), two_row)
            store(sample, one, two)


def attend(qkv, prefix_keys, prefix_values):
    samples = qkv.shape[0] // SEGS
    group = GROUP
    whole = lambda i: (0, 0)
    per = lambda i: (i, 0, 0, 0)
    return pl.pallas_call(
        functools.partial(attend_kernel, group),
        grid=(samples // group,),
        in_specs=[
            pl.BlockSpec((group * SEGS, 3, ROWS, HEAD_DIM), per),
            pl.BlockSpec((PREFIX, HEAD_DIM), whole),
            pl.BlockSpec((AUG, PREFIX), whole),
        ],
        out_specs=pl.BlockSpec((group * SEGS, 2, HEAD_DIM, SEG), per),
        out_shape=jax.ShapeDtypeStruct((samples * SEGS, 2, HEAD_DIM, SEG), jnp.bfloat16),
        scratch_shapes=[
            pltpu.VMEM((group * QUERIES, HEAD_DIM), jnp.bfloat16),
            pltpu.VMEM((AUG, QUERIES), jnp.float32),
        ],
        compiler_params=pltpu.CompilerParams(vmem_limit_bytes=ATTEND_LIMIT),
        cost_estimate=pl.CostEstimate(
            flops=14_000_000_000, bytes_accessed=7_000_000, transcendentals=15_000_000
        ),
        name="attend",
    )(qkv, prefix_keys, prefix_values)


def place_kernel(heads, turned_ref, select_ref, one_ref, two_ref):
    for step, ref in enumerate((one_ref, two_ref)):
        ref[0] = lax.dot_general(
            select_ref[...],
            turned_ref[:, step].reshape(heads * HEAD_DIM, SEG),
            NT,
            preferred_element_type=jnp.float32,
        ).astype(jnp.bfloat16)


def place_outputs(turned, select):
    heads = 16
    count = turned.shape[0]
    shape = jax.ShapeDtypeStruct((1, SEG, count * HEAD_DIM), jnp.bfloat16)
    spec = pl.BlockSpec((1, SEG, heads * HEAD_DIM), lambda i: (0, 0, i))
    return pl.pallas_call(
        functools.partial(place_kernel, heads),
        grid=(count // heads,),
        in_specs=[
            pl.BlockSpec((heads, 2, HEAD_DIM, SEG), lambda i: (i, 0, 0, 0)),
            pl.BlockSpec((SEG, SEG), lambda i: (0, 0)),
        ],
        out_specs=[spec, spec],
        out_shape=[shape, shape],
        compiler_params=pltpu.CompilerParams(vmem_limit_bytes=PLACE_LIMIT),
        name="place",
    )(turned, select)


def row_order(places):
    diagonal = lax.broadcasted_iota(jnp.int32, (REV, REV), 0) == lax.broadcasted_iota(
        jnp.int32, (REV, REV), 1
    )
    column = jnp.sum(jnp.where(diagonal, places, 0), axis=1, keepdims=True)
    rows = lax.broadcasted_iota(jnp.int32, (REV, SEG), 1)
    hits = jnp.where(column == rows, 1, 0)
    below = jnp.where(column < rows, 1, 0)
    rank = rows[:1] - jnp.sum(below, axis=0, keepdims=True)
    rank = jnp.where(jnp.sum(hits, axis=0, keepdims=True) > 0, -1, rank)
    kept = jnp.where(lax.broadcasted_iota(jnp.int32, (KEPT, SEG), 0) == rank, 1, 0)
    return jnp.concatenate([kept, hits], axis=0).astype(jnp.float32)


def prefix_copies(prefix_ref, part_refs, sems):
    me = lax.axis_index("prompt")
    return [
        pltpu.make_async_copy(prefix_ref.at[me ^ flip], ref, sems.at[index])
        for index, (flip, ref) in enumerate(zip(FLIPS, part_refs))
    ]


def pack_kernel(
    heads, places_ref, rows_ref, reveal_ref, prefix_ref, out_ref, select_ref, *rest
):
    *part_refs, order_ref, sems = rest
    copies = prefix_copies(prefix_ref, part_refs, sems)

    @pl.when(pl.program_id(0) == 0)
    def _():
        for copy in copies:
            copy.start()
        order = row_order(places_ref[...])
        order_ref[...] = order.astype(jnp.bfloat16)
        select_ref[...] = order.T.astype(jnp.bfloat16)

    for kind in range(3):
        moved = jnp.dot(order_ref[...], rows_ref[0, kind], preferred_element_type=jnp.float32)
        moved = moved.astype(jnp.bfloat16)
        for head in range(heads):
            lanes = slice(head * HEAD_DIM, (head + 1) * HEAD_DIM)
            out_ref[head, kind, :SEG] = moved[:, lanes]
            out_ref[head, kind, SEG:] = reveal_ref[0, kind, :, lanes]

    @pl.when(pl.program_id(0) == pl.num_programs(0) - 1)
    def _():
        for copy in copies:
            copy.wait()


def pack(places, rows, reveal, prefix):
    heads = 16
    count = rows.shape[3] // HEAD_DIM
    width = heads * HEAD_DIM
    part = jax.ShapeDtypeStruct(prefix.shape[1:], jnp.bfloat16)
    return pl.pallas_call(
        functools.partial(pack_kernel, heads),
        grid=(count // heads,),
        in_specs=[
            pl.BlockSpec((1, REV), lambda i: (0, 0)),
            pl.BlockSpec((1, 3, SEG, width), lambda i: (0, 0, 0, i)),
            pl.BlockSpec((1, 3, REV, width), lambda i: (0, 0, 0, i)),
            pl.BlockSpec(memory_space=pl.ANY),
        ],
        out_specs=[
            pl.BlockSpec((heads, 3, ROWS, HEAD_DIM), lambda i: (i, 0, 0, 0)),
            pl.BlockSpec((SEG, SEG), lambda i: (0, 0)),
        ]
        + [pl.BlockSpec(part.shape, lambda i: (0, 0, 0))] * len(FLIPS),
        out_shape=[
            jax.ShapeDtypeStruct((count, 3, ROWS, HEAD_DIM), jnp.bfloat16),
            jax.ShapeDtypeStruct((SEG, SEG), jnp.bfloat16),
        ]
        + [part] * len(FLIPS),
        scratch_shapes=[
            pltpu.VMEM((SEG, SEG), jnp.bfloat16),
            pltpu.SemaphoreType.DMA((len(FLIPS),)),
        ],
        compiler_params=pltpu.CompilerParams(vmem_limit_bytes=VMEM_LIMIT),
        name="pack",
    )(places, rows, reveal, prefix)


def prefix_kernel(*refs):
    *parts, prefix_ref, keys_ref, values_ref, own_ref, sem = refs
    copy = pltpu.make_async_copy(prefix_ref.at[lax.axis_index("prompt")], own_ref, sem)
    copy.start()
    values_ref[HEAD_DIM:] = jnp.ones((AUG - HEAD_DIM, PREFIX), jnp.bfloat16)
    count = own_ref.shape[0]
    for index, part in enumerate((*parts, own_ref)):
        if part is own_ref:
            copy.wait()
        span = slice(index * count, (index + 1) * count)
        keys_ref[span] = part[:, 0]
        values_ref[:HEAD_DIM, span] = part[:, 1].T


def arrange_prefix(parts, prefix):
    vmem = pl.BlockSpec(memory_space=pltpu.VMEM)
    return pl.pallas_call(
        prefix_kernel,
        in_specs=[vmem] * len(parts) + [pl.BlockSpec(memory_space=pl.ANY)],
        out_specs=[vmem] * 2,
        out_shape=[
            jax.ShapeDtypeStruct((PREFIX, HEAD_DIM), jnp.bfloat16),
            jax.ShapeDtypeStruct((AUG, PREFIX), jnp.bfloat16),
        ],
        scratch_shapes=[
            pltpu.VMEM(prefix.shape[1:], jnp.bfloat16),
            pltpu.SemaphoreType.DMA,
        ],
        compiler_params=pltpu.CompilerParams(vmem_limit_bytes=PLACE_LIMIT),
        cost_estimate=pl.CostEstimate(
            flops=PREFIX_COST, bytes_accessed=2_000_000, transcendentals=0
        ),
        name="prefix",
    )(*parts, prefix)


def exchange(array):
    return lax.all_to_all(array, "sample", split_axis=0, concat_axis=0, tiled=True)


def trade(part, flip):
    return lax.ppermute(part, "prompt", [(i, i ^ flip) for i in range(4)])


def local(answer_qkv, prefix_kv, reveal_qkv, reveal_places):
    packed, select, *parts = pack(
        reveal_places.reshape(1, REV),
        answer_qkv.transpose(0, 2, 1, 3),
        reveal_qkv.transpose(0, 2, 1, 3),
        prefix_kv,
    )
    parts = [trade(part, flip) for part, flip in zip(parts, FLIPS)]
    grouped = exchange(packed)
    turned = exchange(attend(grouped, *arrange_prefix(parts, prefix_kv)))
    return place_outputs(turned, select)


def solution(mesh):
    placed = (
        P("prompt", "sample", None, None),
        P(None, "prompt", None, "sample"),
        P("prompt", "sample", None, None),
        P("prompt", "sample", None),
    )
    return jax.shard_map(
        local,
        mesh=mesh,
        in_specs=placed,
        out_specs=(P("prompt", "sample", None), P("prompt", "sample", None)),
        check_vma=False,
    )
```

```python
import functools
import math

import jax
import jax.numpy as jnp
from jax import lax
from jax.experimental import pallas as pl
from jax.experimental.pallas import tpu as pltpu
from jax.sharding import PartitionSpec as P

HEAD_DIM = 128
ANS = 1024
SEG = 128
REV = 16
KEPT = SEG - REV
ROWS = SEG + REV
SEGS = ANS // SEG
QUERIES = SEGS * ROWS
PREFIX = 2048
CHUNK = 512
RATE = math.log2(math.e) / math.sqrt(HEAD_DIM)
LIMIT = 100.0
AUG = HEAD_DIM + 16
NT = (((1,), (1,)), ((), ()))
FLIPS = (3, 2, 1)
VMEM_LIMIT = 63 * 2**20
FIRST = 128
SPAN = 4
GROUP = 2
PLACE_LIMIT = 20 * 2**20
ATTEND_LIMIT = 44 * 2**20
PREFIX_COST = 60_000_000_000


def scores_of(keys, queries):
    return lax.dot_general(keys, queries, NT, preferred_element_type=jnp.float32)


def fold_max(scores):
    return jnp.max(scores.reshape(-1, 8, scores.shape[1]), axis=0)


def weigh(scores, reference_row):
    return jnp.exp2((scores - reference_row) * RATE).astype(jnp.bfloat16)


def attend_kernel(group, qkv_ref, prefix_ref, out_ref, queries_ref, total_ref):
    for sample in range(group):
        segs = slice(sample * SEGS, (sample + 1) * SEGS)
        at = sample * QUERIES
        queries_ref[at : at + SEGS * SEG] = qkv_ref[segs, 0, :SEG].reshape(-1, HEAD_DIM)
        queries_ref[at + SEGS * SEG : at + QUERIES] = qkv_ref[segs, 0, SEG:].reshape(-1, HEAD_DIM)

    def weighted(values, weights):
        ones = jnp.ones((AUG - HEAD_DIM, values.shape[0]), jnp.bfloat16)
        turned = jnp.concatenate([values.T, ones], axis=0)
        return jnp.dot(turned, weights, preferred_element_type=jnp.float32)

    def answer_rows(kind, first_seg, segs, rows):
        return qkv_ref[first_seg : first_seg + segs, kind, rows].reshape(-1, HEAD_DIM)

    def step(sample, total, rows, row):
        queries = queries_ref[sample * QUERIES : (sample + 1) * QUERIES]
        scores = scores_of(answer_rows(1, sample * SEGS, SEGS, rows), queries)
        own = weighted(answer_rows(2, sample * SEGS, SEGS, rows), weigh(scores, row)) + total
        return own[:HEAD_DIM] * (1.0 / own[HEAD_DIM : HEAD_DIM + 1]), fold_max(scores)

    def store(sample, one, two):
        renewed = two[:, SEGS * SEG :]
        lane = lax.broadcasted_iota(jnp.int32, (HEAD_DIM, SEG), 1)
        for seg in range(SEGS):
            lanes = slice(seg * SEG, (seg + 1) * SEG)
            out_ref[sample * SEGS + seg, 0] = one[:, lanes].astype(jnp.bfloat16)
            shift = (KEPT - seg * REV) % SEG
            moved = pltpu.roll(renewed, shift, 1) if shift else renewed
            merged = jnp.where(lane < KEPT, two[:, lanes], moved)
            out_ref[sample * SEGS + seg, 1] = merged.astype(jnp.bfloat16)

    queries = queries_ref[...]
    start_row = jnp.max(scores_of(prefix_ref[0, :FIRST], queries), axis=0, keepdims=True)
    prefix_total = None
    prefix_max = None
    for start in range(0, PREFIX, CHUNK):
        scores = scores_of(prefix_ref[0, start : start + CHUNK], queries)
        folded = fold_max(scores)
        prefix_max = folded if prefix_max is None else jnp.maximum(prefix_max, folded)
        part = weighted(prefix_ref[1, start : start + CHUNK], weigh(scores, start_row))
        prefix_total = part if prefix_total is None else prefix_total + part

    largest = []
    excess = None
    for sample in range(group):
        lanes = slice(sample * QUERIES, (sample + 1) * QUERIES)
        row = start_row[:, lanes]
        total = prefix_total[:, lanes]
        common_max = prefix_max[:, lanes]
        for start in range(0, SEGS, SPAN):
            first_seg = sample * SEGS + start
            scores = scores_of(answer_rows(1, first_seg, SPAN, slice(0, KEPT)), queries[lanes])
            common_max = jnp.maximum(common_max, fold_max(scores))
            total += weighted(
                answer_rows(2, first_seg, SPAN, slice(0, KEPT)), weigh(scores, row)
            )
        one, one_max = step(sample, total, slice(KEPT, SEG), row)
        two, two_max = step(sample, total, slice(SEG, ROWS), row)
        store(sample, one, two)
        largest.append((common_max, one_max, two_max))
        above = jnp.maximum(common_max, jnp.maximum(one_max, two_max)) - row
        excess = above if excess is None else jnp.maximum(excess, above)

    @pl.when(jnp.max(excess) * RATE > LIMIT)
    def _():
        for sample, (common_max, one_max, two_max) in enumerate(largest):
            rows = slice(sample * QUERIES, (sample + 1) * QUERIES)
            common_row = jnp.max(common_max, axis=0, keepdims=True)
            one_row = jnp.maximum(common_row, jnp.max(one_max, axis=0, keepdims=True))
            two_row = jnp.maximum(common_row, jnp.max(two_max, axis=0, keepdims=True))
            total_ref[...] = jnp.zeros_like(total_ref)

            def add_prefix(index, carry):
                span = pl.ds(pl.multiple_of(index * FIRST, FIRST), FIRST)
                weights = weigh(scores_of(prefix_ref[0, span], queries_ref[rows]), common_row)
                total_ref[...] += weighted(prefix_ref[1, span], weights)
                return carry

            def add_answers(seg, carry):
                scores = scores_of(qkv_ref[seg, 1, :KEPT], queries_ref[rows])
                total_ref[...] += weighted(qkv_ref[seg, 2, :KEPT], weigh(scores, common_row))
                return carry

            lax.fori_loop(0, PREFIX // FIRST, add_prefix, 0)
            lax.fori_loop(sample * SEGS, (sample + 1) * SEGS, add_answers, 0)
            scale_one = jnp.exp2((common_row - one_row) * RATE)
            scale_two = jnp.exp2((common_row - two_row) * RATE)
            one, _ = step(sample, total_ref[...] * scale_one, slice(KEPT, SEG), one_row)
            two, _ = step(sample, total_ref[...] * scale_two, slice(SEG, ROWS), two_row)
            store(sample, one, two)


def attend(qkv, prefix):
    samples = qkv.shape[0] // SEGS
    group = GROUP
    per = lambda i: (i, 0, 0, 0)
    return pl.pallas_call(
        functools.partial(attend_kernel, group),
        grid=(samples // group,),
        in_specs=[
            pl.BlockSpec((group * SEGS, 3, ROWS, HEAD_DIM), per),
            pl.BlockSpec((2, PREFIX, HEAD_DIM), lambda i: (0, 0, 0)),
        ],
        out_specs=pl.BlockSpec((group * SEGS, 2, HEAD_DIM, SEG), per),
        out_shape=jax.ShapeDtypeStruct((samples * SEGS, 2, HEAD_DIM, SEG), jnp.bfloat16),
        scratch_shapes=[
            pltpu.VMEM((group * QUERIES, HEAD_DIM), jnp.bfloat16),
            pltpu.VMEM((AUG, QUERIES), jnp.float32),
        ],
        compiler_params=pltpu.CompilerParams(vmem_limit_bytes=ATTEND_LIMIT),
        cost_estimate=pl.CostEstimate(
            flops=14_000_000_000, bytes_accessed=7_000_000, transcendentals=15_000_000
        ),
        name="attend",
    )(qkv, prefix)


def place_kernel(heads, turned_ref, select_ref, one_ref, two_ref):
    for step, ref in enumerate((one_ref, two_ref)):
        ref[0] = lax.dot_general(
            select_ref[...],
            turned_ref[:, step].reshape(heads * HEAD_DIM, SEG),
            NT,
            preferred_element_type=jnp.float32,
        ).astype(jnp.bfloat16)


def place_outputs(turned, select):
    heads = 16
    count = turned.shape[0]
    shape = jax.ShapeDtypeStruct((1, SEG, count * HEAD_DIM), jnp.bfloat16)
    spec = pl.BlockSpec((1, SEG, heads * HEAD_DIM), lambda i: (0, 0, i))
    return pl.pallas_call(
        functools.partial(place_kernel, heads),
        grid=(count // heads,),
        in_specs=[
            pl.BlockSpec((heads, 2, HEAD_DIM, SEG), lambda i: (i, 0, 0, 0)),
            pl.BlockSpec((SEG, SEG), lambda i: (0, 0)),
        ],
        out_specs=[spec, spec],
        out_shape=[shape, shape],
        compiler_params=pltpu.CompilerParams(vmem_limit_bytes=PLACE_LIMIT),
        name="place",
    )(turned, select)


def row_order(places):
    diagonal = lax.broadcasted_iota(jnp.int32, (REV, REV), 0) == lax.broadcasted_iota(
        jnp.int32, (REV, REV), 1
    )
    column = jnp.sum(jnp.where(diagonal, places, 0), axis=1, keepdims=True)
    rows = lax.broadcasted_iota(jnp.int32, (REV, SEG), 1)
    hits = jnp.where(column == rows, 1, 0)
    below = jnp.where(column < rows, 1, 0)
    rank = rows[:1] - jnp.sum(below, axis=0, keepdims=True)
    rank = jnp.where(jnp.sum(hits, axis=0, keepdims=True) > 0, -1, rank)
    kept = jnp.where(lax.broadcasted_iota(jnp.int32, (KEPT, SEG), 0) == rank, 1, 0)
    return jnp.concatenate([kept, hits], axis=0).astype(jnp.float32)


def prefix_copies(prefix_ref, part_refs, sems):
    me = lax.axis_index("prompt")
    return [
        pltpu.make_async_copy(prefix_ref.at[me ^ flip], ref, sems.at[index])
        for index, (flip, ref) in enumerate(zip(FLIPS, part_refs))
    ]


def pack_kernel(
    heads, places_ref, rows_ref, reveal_ref, prefix_ref, out_ref, select_ref, *rest
):
    *part_refs, order_ref, sems = rest
    copies = prefix_copies(prefix_ref, part_refs, sems)

    @pl.when(pl.program_id(0) == 0)
    def _():
        for copy in copies:
            copy.start()
        order = row_order(places_ref[...])
        order_ref[...] = order.astype(jnp.bfloat16)
        select_ref[...] = order.T.astype(jnp.bfloat16)

    for kind in range(3):
        moved = jnp.dot(order_ref[...], rows_ref[0, kind], preferred_element_type=jnp.float32)
        moved = moved.astype(jnp.bfloat16)
        for head in range(heads):
            lanes = slice(head * HEAD_DIM, (head + 1) * HEAD_DIM)
            out_ref[head, kind, :SEG] = moved[:, lanes]
            out_ref[head, kind, SEG:] = reveal_ref[0, kind, :, lanes]

    @pl.when(pl.program_id(0) == pl.num_programs(0) - 1)
    def _():
        for copy in copies:
            copy.wait()


def pack(places, rows, reveal, prefix):
    heads = 16
    count = rows.shape[3] // HEAD_DIM
    width = heads * HEAD_DIM
    part = jax.ShapeDtypeStruct(prefix.shape[1:], jnp.bfloat16)
    return pl.pallas_call(
        functools.partial(pack_kernel, heads),
        grid=(count // heads,),
        in_specs=[
            pl.BlockSpec((1, REV), lambda i: (0, 0)),
            pl.BlockSpec((1, 3, SEG, width), lambda i: (0, 0, 0, i)),
            pl.BlockSpec((1, 3, REV, width), lambda i: (0, 0, 0, i)),
            pl.BlockSpec(memory_space=pl.ANY),
        ],
        out_specs=[
            pl.BlockSpec((heads, 3, ROWS, HEAD_DIM), lambda i: (i, 0, 0, 0)),
            pl.BlockSpec((SEG, SEG), lambda i: (0, 0)),
        ]
        + [pl.BlockSpec(part.shape, lambda i: (0, 0, 0))] * len(FLIPS),
        out_shape=[
            jax.ShapeDtypeStruct((count, 3, ROWS, HEAD_DIM), jnp.bfloat16),
            jax.ShapeDtypeStruct((SEG, SEG), jnp.bfloat16),
        ]
        + [part] * len(FLIPS),
        scratch_shapes=[
            pltpu.VMEM((SEG, SEG), jnp.bfloat16),
            pltpu.SemaphoreType.DMA((len(FLIPS),)),
        ],
        compiler_params=pltpu.CompilerParams(vmem_limit_bytes=VMEM_LIMIT),
        name="pack",
    )(places, rows, reveal, prefix)


def prefix_kernel(*refs):
    *parts, prefix_ref, out_ref, own_ref, sem = refs
    copy = pltpu.make_async_copy(prefix_ref.at[lax.axis_index("prompt")], own_ref, sem)
    copy.start()
    count = own_ref.shape[0]
    for index, part in enumerate((*parts, own_ref)):
        if part is own_ref:
            copy.wait()
        span = slice(index * count, (index + 1) * count)
        out_ref[0, span] = part[:, 0]
        out_ref[1, span] = part[:, 1]


def arrange_prefix(parts, prefix):
    vmem = pl.BlockSpec(memory_space=pltpu.VMEM)
    return pl.pallas_call(
        prefix_kernel,
        in_specs=[vmem] * len(parts) + [pl.BlockSpec(memory_space=pl.ANY)],
        out_specs=vmem,
        out_shape=jax.ShapeDtypeStruct((2, PREFIX, HEAD_DIM), jnp.bfloat16),
        scratch_shapes=[
            pltpu.VMEM(prefix.shape[1:], jnp.bfloat16),
            pltpu.SemaphoreType.DMA,
        ],
        compiler_params=pltpu.CompilerParams(vmem_limit_bytes=PLACE_LIMIT),
        cost_estimate=pl.CostEstimate(
            flops=PREFIX_COST, bytes_accessed=2_000_000, transcendentals=0
        ),
        name="prefix",
    )(*parts, prefix)


def exchange(array):
    return lax.all_to_all(array, "sample", split_axis=0, concat_axis=0, tiled=True)


def trade(part, flip):
    return lax.ppermute(part, "prompt", [(i, i ^ flip) for i in range(4)])


def local(answer_qkv, prefix_kv, reveal_qkv, reveal_places):
    packed, select, *parts = pack(
        reveal_places.reshape(1, REV),
        answer_qkv.transpose(0, 2, 1, 3),
        reveal_qkv.transpose(0, 2, 1, 3),
        prefix_kv,
    )
    parts = [trade(part, flip) for part, flip in zip(parts, FLIPS)]
    grouped = exchange(packed)
    turned = exchange(attend(grouped, arrange_prefix(parts, prefix_kv)))
    return place_outputs(turned, select)


def solution(mesh):
    placed = (
        P("prompt", "sample", None, None),
        P(None, "prompt", None, "sample"),
        P("prompt", "sample", None, None),
        P("prompt", "sample", None),
    )
    return jax.shard_map(
        local,
        mesh=mesh,
        in_specs=placed,
        out_specs=(P("prompt", "sample", None), P("prompt", "sample", None)),
        check_vma=False,
    )
```
